32 devices in a mesh: term: 16 (over z, y, x), sector: 2 (over core).
Axes of the slice: x: 2, y: 2, z: 4, core: 2. Of those that a mesh axis runs over, the one named last changes fastest.
Arguments:
- wave_blocks: bfloat16 [4, 512, 512], P(None, 'term'), may hold values from -0.59765625 to 0.59765625
- left_ops: bfloat16 [2, 32, 512, 512], P('sector', 'term'), may hold values from -0.25 to 0.25
- right_ops: bfloat16 [2, 64, 512, 512], P('sector', 'term'), may hold values from -0.25 to 0.25
- wanted: int32 [2, 16, 2], P('sector'), may hold values from 0 to 3, as said below
- pairs: int32 [2, 16, 12], P('sector', 'term'), may hold values from 0 to 15, as said below
- targets: int32 [2, 16, 12], P('sector', 'term'), may hold values from 0 to 1
- live: int32 [2, 16], P('sector', 'term'), may hold values from 1 to 12, as said below
Outputs:
- sigma: float32 [4, 512, 512], P('sector', 'term')
The draws below stay inside these ranges and needn't reach their ends.
Inputs may be any that keep to these rules, and one draw needn't show every extreme that they name: `wanted`: the sectors listed for one section are distinct. `pairs`: codes are distinct within a section; a code c names half product c // 4 and right operator c % 4 of the section. Only the first live slots of a section are used; in every draw some section has 12 live slots.
All inputs are finite; a program needn't handle non-finite values.
Results may differ from the reference program's by a relative error of at most 0.0029.
Values may be sent and summed in bfloat16 or wider, within the bound.
No kernel may reach another device: no remote copies, remote signals or barrier semaphores. Data moves between devices by JAX's collectives and lax.ppermute only.
A program may use at most 64 MiB of HBM per device.

```python
import jax
import jax.numpy as jnp
from jax import lax

B = 512
SEC_DEV = 2
NEED_DEV = 2
OPS_L = 2
OPS_R = 4
TERM_DEV = 12
GROUPS = 2
SECTIONS = 16
SECTORS = 4
HALVES = 4


def pick_distinct(key, pool, taken):
    keys = jax.random.split(key, GROUPS * SECTIONS)

    def one_pick(one_key):
        return jax.random.permutation(one_key, pool)[:taken]
    picks = jax.vmap(one_pick)(keys)
    return picks.reshape(GROUPS, SECTIONS, taken).astype(jnp.int32)


def draw_wanted(key, part):
    return pick_distinct(jax.random.fold_in(key, 11), SECTORS, NEED_DEV)


def draw_pairs(key, part):
    return pick_distinct(jax.random.fold_in(key, 23), HALVES * OPS_R, TERM_DEV)


def draw_live(key, part):
    first_key = jax.random.fold_in(key, 37)
    second_key = jax.random.fold_in(key, 41)
    counts = jax.random.randint(first_key, (GROUPS * SECTIONS,), 1, TERM_DEV + 1)
    fullest = jax.random.randint(second_key, (), 0, GROUPS * SECTIONS)
    counts = counts.at[fullest].set(TERM_DEV)
    return counts.reshape(GROUPS, SECTIONS).astype(jnp.int32)


def plant(drawn, key, smallest, top_value):
    dims = drawn.shape
    spot = [jax.random.randint(jax.random.fold_in(key, axis), (), 0, dims[axis]) for axis in range(len(dims))]
    drawn = drawn.at[tuple(spot)].set(smallest)
    longest = dims.index(max(dims))
    spot[longest] = (spot[longest] + 1) % dims[longest]
    return drawn.at[tuple(spot)].set(top_value)


def levels(own_key, dims, cuts, least, largest):
    def one(position, shards_of):
        draws = jax.random.uniform(jax.random.fold_in(jax.random.fold_in(own_key, 6), position), (shards_of,), jnp.float32, least / len(cuts), largest / len(cuts))
        return jnp.repeat(jnp.exp(draws), dims[position] // shards_of).reshape((-1,) + (1,) * (len(dims) - position - 1))

    level = one(*cuts[0])
    for cut in cuts[1:]:
        level = level * one(*cut)
    return level


def noise(key, shape, deviation, most, shards=(), kind=jnp.bfloat16):
    loudness = levels(key, shape, shards, -0.22, 0.18) if shards else 1.0
    result = jax.random.normal(key, shape, jnp.float32) * deviation * loudness
    return jnp.minimum(jnp.maximum(result, -most), most).astype(kind)


def setup_inputs(seed: int = 0) -> dict:
    seeds = jax.random.split(jax.random.key(seed), 8)
    return {
        "wave_blocks": noise(seeds[0], (SECTORS, B, B), 0.1, 0.59765625, ((1, 16),)),
        "left_ops": noise(seeds[1], (GROUPS, SECTIONS * OPS_L, B, B), B ** -0.5, 0.25, ((0, 2), (1, 16))),
        "right_ops": noise(seeds[2], (GROUPS, SECTIONS * OPS_R, B, B), B ** -0.5, 0.25, ((0, 2), (1, 16))),
        "wanted": draw_wanted(jax.random.fold_in(seeds[7], 71), 0),
        "pairs": draw_pairs(jax.random.fold_in(seeds[7], 71), 0),
        "targets": plant(jax.random.randint(seeds[5], (GROUPS, SECTIONS, TERM_DEV), 0, SEC_DEV), jax.random.fold_in(seeds[5], 1), 0, SEC_DEV - 1).astype(jnp.int32),
        "live": draw_live(jax.random.fold_in(seeds[7], 71), 0),
    }


def reference(wave_blocks, left_ops, right_ops, wanted, pairs, targets, live):
    highest = lax.Precision.HIGHEST
    wave_wide = wave_blocks.astype(jnp.float32)
    sigma_start = jnp.zeros((SECTORS, B, B), jnp.float32)

    def device_step(sigma, device_flat):
        group_index = device_flat // SECTIONS
        section_index = device_flat % SECTIONS
        lefts = lax.dynamic_slice_in_dim(left_ops[group_index], section_index * OPS_L, OPS_L, 0).astype(jnp.float32)
        rights = lax.dynamic_slice_in_dim(right_ops[group_index], section_index * OPS_R, OPS_R, 0).astype(jnp.float32)
        sources = wanted[group_index, section_index].astype(jnp.int32)
        blocks = jnp.take(wave_wide, sources, axis=0)
        halves = jnp.einsum("aij,njk->anik", lefts, blocks, precision=highest)
        halves = lax.optimization_barrier(halves.astype(jnp.bfloat16)).astype(jnp.float32)
        halves = halves.reshape(HALVES, B, B)

        def slot_step(sigma_now, slot):
            pair_code = pairs[group_index, section_index, slot]
            product = jnp.dot(halves[pair_code // OPS_R], rights[pair_code % OPS_R].T, precision=highest)
            weight = (slot < live[group_index, section_index]).astype(jnp.float32)
            owner = (group_index * SEC_DEV + targets[group_index, section_index, slot]).astype(jnp.int32)
            current = lax.dynamic_index_in_dim(sigma_now, owner, 0, keepdims=False)
            sigma_now = lax.dynamic_update_index_in_dim(sigma_now, current + weight * product, owner, 0)
            return sigma_now, None

        sigma, unused = lax.scan(slot_step, sigma, jnp.arange(TERM_DEV, dtype=jnp.int32))
        return sigma, None

    sigma, unused = lax.scan(device_step, sigma_start, jnp.arange(GROUPS * SECTIONS, dtype=jnp.int32))
    return sigma
```

```python
import functools

import jax
import jax.numpy as jnp
from jax import lax
from jax.experimental import pallas as pl
from jax.experimental.pallas import tpu as pltpu
from jax.sharding import PartitionSpec as P

AXES = ("term", "sector")
BF16 = jnp.bfloat16
F32 = jnp.float32
VMEM = pl.BlockSpec(memory_space=pltpu.VMEM)
SMEM = pl.BlockSpec(memory_space=pltpu.SMEM)
VMEM_BYTES = 24 * 2**20


def block_owner(position, me, core, depth):
    quarter, level = position // depth, position % depth
    swapped = (0, 2, 1, 3)[quarter]
    near = jnp.where(core == 0, quarter, swapped)
    return lax.bitwise_xor(me, near + 4 * level)


def sigma_kernel(place, wanted, pairs, targets, live, mine, other, left, right,
                 keep0, send1, keep2, send3, wave, halves, total):
    devices, half_sectors, rows, size = mine.shape
    depth = devices // 4
    ops_l, ops_r, need = left.shape[1], right.shape[1], wave.shape[0]
    me, core = place[0], place[1]

    for j in range(need):
        source = wanted[0, me, j]
        owner_core = source // half_sectors
        local = source % half_sectors

        def unpack(blocks, from_core):
            for position in range(devices):
                start = block_owner(position, me, from_core, depth) * rows
                wave[j, pl.ds(pl.multiple_of(start, rows), rows), :] = blocks[position, local].astype(wave.dtype)

        @pl.when(owner_core == core)
        def _():
            unpack(mine, core)

        @pl.when(owner_core != core)
        def _():
            unpack(other, 1 - core)

    for a in range(ops_l):
        for j in range(need):
            product = jnp.dot(left[0, a], wave[j].astype(BF16), preferred_element_type=F32)
            halves[a * need + j] = product.astype(BF16)

    total[...] = jnp.zeros_like(total)

    def slot_step(slot, carry):
        code = pairs[0, 0, slot]
        target = targets[0, 0, slot]
        total[target] += lax.dot_general(
            halves[code // ops_r], right[0, code % ops_r], (((1,), (1,)), ((), ())), preferred_element_type=F32
        )
        return carry

    lax.fori_loop(0, live[0, 0], slot_step, 0)

    for quarter, out in enumerate((keep0, send1, keep2, send3)):
        for level in range(depth):
            start = block_owner(quarter * depth + level, me, core, depth) * rows
            for t in range(total.shape[0]):
                out[level, t] = total[t, pl.ds(pl.multiple_of(start, rows), rows), :].astype(out.dtype)


def on_device(terms, cores, wave_blocks, left_ops, right_ops, wanted, pairs, targets, live):
    sectors, rows, size = wave_blocks.shape
    me = lax.axis_index("term")
    core = lax.axis_index("sector") % 2
    depth = terms // 4
    sec_dev = sectors // cores
    need = wanted.shape[2]

    def swap(array, near, level=0):
        def partner(t, c):
            return t ^ (near[c % 2] + 4 * level)
        pairs_of = [(t * cores + c, partner(t, c) * cores + c) for t in range(terms) for c in range(cores)]
        return lax.ppermute(array, AXES, pairs_of)

    none, first, second = (0, 0), (1, 2), (2, 1)
    across = [(t * cores + c, t * cores + (c ^ 1)) for t in range(terms) for c in range(cores)]

    half = sectors // 2
    own = lax.dynamic_slice_in_dim(wave_blocks, core * half, half, 0)[None]
    line = jnp.concatenate([own] + [swap(own, none, k) for k in range(1, depth)], 0)
    from_first = swap(line, first)
    from_second = swap(line, second)
    from_both = swap(from_first, second)
    mine = jnp.concatenate([line, from_first, from_second, from_both], 0)
    other = lax.ppermute(mine, AXES, across)

    place = jnp.stack([me, core]).astype(jnp.int32)
    blocks = (depth, sec_dev, rows, size)
    wave_type = BF16 if rows % 16 == 0 else F32
    keep0, send1, keep2, send3 = pl.pallas_call(
        sigma_kernel,
        out_shape=[jax.ShapeDtypeStruct(blocks, t) for t in (F32, BF16, F32, BF16)],
        in_specs=[SMEM] * 5 + [VMEM] * 4,
        out_specs=[VMEM] * 4,
        scratch_shapes=[
            pltpu.VMEM((need, size, size), wave_type),
            pltpu.VMEM((left_ops.shape[1] * need, size, size), BF16),
            pltpu.VMEM((sec_dev, size, size), F32),
        ],
        compiler_params=pltpu.CompilerParams(vmem_limit_bytes=VMEM_BYTES),
        cost_estimate=pl.CostEstimate(flops=32 * size**3, bytes_accessed=12 * size * size * 2, transcendentals=0),
    )(place, wanted, pairs, targets, live, mine, other, left_ops, right_ops)

    far = swap(send3, first)
    near = swap(send1, first)
    passed = swap((keep2 + far.astype(F32)).astype(BF16), second)
    line_sum = keep0 + near.astype(F32) + passed.astype(F32)
    arrived = [swap(line_sum[k].astype(BF16), none, k) for k in range(1, depth)]
    sigma = line_sum[0]
    for part in arrived:
        sigma = sigma + part.astype(F32)
    return sigma


def solution(mesh):
    return jax.shard_map(
        functools.partial(on_device, mesh.shape["term"], mesh.shape["sector"]),
        mesh=mesh,
        in_specs=(
            P(None, "term", None),
            P("sector", "term", None, None),
            P("sector", "term", None, None),
            P("sector", None, None),
            P("sector", "term", None),
            P("sector", "term", None),
            P("sector", "term"),
        ),
        out_specs=P("sector", "term", None),
        check_vma=False,
    )
```

```python
import functools

import jax
import jax.numpy as jnp
from jax import lax
from jax.experimental import pallas as pl
from jax.experimental.pallas import tpu as pltpu
from jax.sharding import PartitionSpec as P

AXES = ("term", "sector")
BF16 = jnp.bfloat16
F32 = jnp.float32
VMEM = pl.BlockSpec(memory_space=pltpu.VMEM)
SMEM = pl.BlockSpec(memory_space=pltpu.SMEM)
VMEM_BYTES = 24 * 2**20
GROUPS = ((3,), (1,), (2, 0))


def block_rows(me, core, quarter, level, rows):
    near = jnp.where(core == 0, quarter, (0, 2, 1, 3)[quarter])
    owner = lax.bitwise_xor(me, near + 4 * level)
    return pl.ds(pl.multiple_of(owner * rows, rows), rows)


def prepare_kernel(rows, place, wanted, left, right, *refs):
    lefts, lasts = refs[:len(GROUPS)], refs[len(GROUPS):2 * len(GROUPS)]
    turned, sources, flipped, picked = refs[2 * len(GROUPS):]
    me, core = place[0], place[1]
    depth = left.shape[2] // (4 * rows)
    sources[0], sources[1] = me, core
    for j in range(wanted.shape[2]):
        sources[2 + j] = wanted[0, me, j]
    for a in range(left.shape[1]):
        for out, last, quarters in zip(lefts, lasts, GROUPS):
            used = out.shape[1]
            for i, quarter in enumerate(quarters):
                for level in range(depth):
                    window = block_rows(me, core, quarter, level, rows)
                    out[a, pl.ds((i * depth + level) * rows, rows), :] = left[0, a, window, :]
            flipped[:, :used] = out[a].T
            for level in range(depth):
                window = block_rows(me, core, 3, level, rows)
                picked[pl.ds(level * rows, rows), :used] = flipped[window, :used]
            last[a] = picked[:, :used].T
    for r in range(right.shape[1]):
        turned[r] = right[0, r].T


def early_kernel(sources, mine, other, *refs):
    lefts, sums, wave = refs[:len(GROUPS)], refs[len(GROUPS):2 * len(GROUPS)], refs[-1]
    half_sectors, rows = mine.shape[1], mine.shape[2]
    depth = mine.shape[0] // 3
    me, core = sources[0], sources[1]
    for j in range(wave.shape[0]):
        source = sources[2 + j]
        for level in range(depth):
            window = block_rows(me, core, 3, level, rows)
            wave[j, window, :] = jnp.zeros((rows, wave.shape[2]), wave.dtype)

        def unpack(blocks, from_core):
            for quarter in range(3):
                for level in range(depth):
                    block = blocks[quarter * depth + level, source % half_sectors]
                    wave[j, block_rows(me, from_core, quarter, level, rows), :] = block.astype(wave.dtype)

        @pl.when(source // half_sectors == core)
        def _():
            unpack(mine, core)

        @pl.when(source // half_sectors != core)
        def _():
            unpack(other, 1 - core)

    for left, out in zip(lefts, sums):
        for a in range(left.shape[0]):
            for j in range(wave.shape[0]):
                out[a * wave.shape[0] + j] = jnp.dot(
                    left[a].astype(BF16), wave[j].astype(BF16), preferred_element_type=F32
                )


def products(pairs, targets, live, early, left_last, wave_last, turned, outs, halves, total):
    ops_r, need = turned.shape[0], wave_last.shape[0]
    for a in range(left_last.shape[0]):
        for j in range(need):
            late = jnp.dot(left_last[a].astype(BF16), wave_last[j].astype(BF16), preferred_element_type=F32)
            halves[a * need + j] = (early[a * need + j] + late).astype(BF16)

    total[...] = jnp.zeros_like(total)
    for slot in range(pairs.shape[2]):
        code = pairs[0, 0, slot]
        target = jnp.where(slot < live[0, 0], targets[0, 0, slot], total.shape[0] - 1)
        total[target] += jnp.dot(halves[code // ops_r], turned[code % ops_r], preferred_element_type=F32)

    for i, out in enumerate(outs):
        depth, sec_dev, rows = out.shape[:3]
        for level in range(depth):
            for t in range(sec_dev):
                out[level, t] = total[t, pl.ds((i * depth + level) * rows, rows), :].astype(out.dtype)


def first_kernel(sources, pairs, targets, live, mine_last, other_last, early, left_last, turned,
                 wave_last, out, halves, total):
    depth, half_sectors, rows, size = mine_last.shape
    for j in range(wave_last.shape[0]):
        source = sources[2 + j]
        for owned, blocks in ((True, mine_last), (False, other_last)):
            @pl.when((source // half_sectors == sources[1]) == owned)
            def _(blocks=blocks):
                for level in range(depth):
                    block = blocks[level, source % half_sectors]
                    wave_last[j, pl.ds(level * rows, rows), :] = block.astype(wave_last.dtype)

    products(pairs, targets, live, early, left_last, wave_last, turned, [out], halves, total)


def next_kernel(pairs, targets, live, early, left_last, wave_last, turned, *refs):
    products(pairs, targets, live, early, left_last, wave_last, turned, refs[:-2], *refs[-2:])


def call(kernel, out_shapes, scratch_shapes, flops, *operands):
    def spec(array):
        return SMEM if jnp.issubdtype(array.dtype, jnp.integer) else VMEM

    return pl.pallas_call(
        kernel,
        out_shape=out_shapes,
        in_specs=[spec(operand) for operand in operands],
        out_specs=[spec(out) for out in out_shapes],
        scratch_shapes=scratch_shapes,
        compiler_params=pltpu.CompilerParams(vmem_limit_bytes=VMEM_BYTES),
        cost_estimate=pl.CostEstimate(flops=flops, bytes_accessed=2**20, transcendentals=0),
    )(*operands)


def on_device(terms, cores, wave_blocks, left_ops, right_ops, wanted, pairs, targets, live):
    sectors, rows, size = wave_blocks.shape
    me = lax.axis_index("term")
    core = lax.axis_index("sector") % 2
    depth = terms // 4
    sec_dev = sectors // cores
    ops_l, ops_r, need = left_ops.shape[1], right_ops.shape[1], wanted.shape[2]
    half = sectors // 2
    quarter = depth * rows
    shape = jax.ShapeDtypeStruct

    def swap(array, near, level=0):
        def partner(t, c):
            return t ^ (near[c % 2] + 4 * level)
        pairs_of = [(t * cores + c, partner(t, c) * cores + c) for t in range(terms) for c in range(cores)]
        return lax.ppermute(array, AXES, pairs_of)

    none, first, second = (0, 0), (1, 2), (2, 1)
    across = [(t * cores + c, t * cores + (c ^ 1)) for t in range(terms) for c in range(cores)]

    work_type = BF16 if rows % 16 == 0 else F32
    used = [len(group) * quarter for group in GROUPS]
    place = jnp.stack([me, core]).astype(jnp.int32)
    *prepared, sources = call(
        functools.partial(prepare_kernel, rows),
        [shape((ops_l, u, size), work_type) for u in used]
        + [shape((ops_l, u, quarter), work_type) for u in used]
        + [shape((ops_r, size, size), BF16), shape((2 + need,), jnp.int32)],
        [pltpu.VMEM((size, max(used)), work_type), pltpu.VMEM((quarter, max(used)), work_type)],
        size**3, place, wanted, left_ops.astype(work_type), right_ops,
    )

    own = lax.dynamic_slice_in_dim(wave_blocks, core * half, half, 0)[None]
    line = jnp.concatenate([own] + [swap(own, none, k) for k in range(1, depth)], 0)
    line, prepared, sources = lax.optimization_barrier((line, prepared, sources))
    lefts, lasts, turned = prepared[:len(GROUPS)], prepared[len(GROUPS):-1], prepared[-1]
    from_first = swap(line, first)
    from_second = swap(line, second)
    mine_last = swap(from_first, second)
    mine = jnp.concatenate([line, from_first, from_second], 0)
    other = lax.ppermute(mine, AXES, across)
    early = call(
        early_kernel,
        [shape((ops_l * need, u, size), F32) for u in used],
        [pltpu.VMEM((need, size, size), work_type)],
        8 * size**3, sources, mine, other, *lefts,
    )
    mine_last, early = lax.optimization_barrier((mine_last, early))
    other_last = lax.ppermute(mine_last, AXES, across)

    def sums(kernel, group, extra, kinds, *operands):
        return call(
            kernel, extra + [shape((depth, sec_dev, rows, size), kind) for kind in kinds],
            [pltpu.VMEM((ops_l * need, used[group], size), BF16), pltpu.VMEM((sec_dev + 1, used[group], size), F32)],
            24 * used[group] * size**2, *operands,
        )

    wave_last, far = sums(
        first_kernel, 0, [shape((need, quarter, size), work_type)], (BF16,),
        sources, pairs, targets, live, mine_last, other_last, early[0], lasts[0], turned,
    )
    far = swap(far, first)
    near, = sums(next_kernel, 1, [], (BF16,), pairs, targets, live, early[1], lasts[1], wave_last, turned)
    near = swap(near, first)
    passing, keep = sums(next_kernel, 2, [], (F32, F32), pairs, targets, live, early[2], lasts[2], wave_last, turned)

    passing = (passing + far.astype(F32)).astype(BF16)
    pass_rest = swap(passing[1:], second)
    line_rest = (keep[1:] + near[1:].astype(F32) + pass_rest.astype(F32)).astype(BF16)
    line_rest, pass_own = lax.optimization_barrier((line_rest, passing[0]))
    arrived = [swap(line_rest[k - 1], none, k) for k in range(1, depth)]
    pass_own = swap(pass_own, second)
    sigma = keep[0] + near[0].astype(F32) + pass_own.astype(F32)
    for part in arrived:
        sigma = sigma + part.astype(F32)
    return sigma


def solution(mesh):
    return jax.shard_map(
        functools.partial(on_device, mesh.shape["term"], mesh.shape["sector"]),
        mesh=mesh,
        in_specs=(
            P(None, "term", None),
            P("sector", "term", None, None),
            P("sector", "term", None, None),
            P("sector", None, None),
            P("sector", "term", None),
            P("sector", "term", None),
            P("sector", "term"),
        ),
        out_specs=P("sector", "term", None),
        check_vma=False,
    )
```

```python
import functools

import jax
import jax.numpy as jnp
from jax import lax
from jax.experimental import pallas as pl
from jax.experimental.pallas import tpu as pltpu
from jax.sharding import PartitionSpec as P

AXES = ("term", "sector")
BF16 = jnp.bfloat16
F32 = jnp.float32
VMEM = pl.BlockSpec(memory_space=pltpu.VMEM)
SMEM = pl.BlockSpec(memory_space=pltpu.SMEM)
VMEM_BYTES = 24 * 2**20
GROUPS = ((3,), (1,), (2, 0))


def block_rows(me, core, quarter, level, rows):
    near = jnp.where(core == 0, quarter, (0, 2, 1, 3)[quarter])
    owner = lax.bitwise_xor(me, near + 4 * level)
    return pl.ds(pl.multiple_of(owner * rows, rows), rows)


def prepare_kernel(rows, place, wanted, left, right, *refs):
    lefts, lasts = refs[:len(GROUPS)], refs[len(GROUPS):2 * len(GROUPS)]
    turned, sources, flipped, picked = refs[2 * len(GROUPS):]
    me, core = place[0], place[1]
    depth = left.shape[2] // (4 * rows)
    sources[0], sources[1] = me, core
    for j in range(wanted.shape[2]):
        sources[2 + j] = wanted[0, me, j]
    for a in range(left.shape[1]):
        for out, last, quarters in zip(lefts, lasts, GROUPS):
            used = out.shape[1]
            for i, quarter in enumerate(quarters):
                for level in range(depth):
                    window = block_rows(me, core, quarter, level, rows)
                    out[a, pl.ds((i * depth + level) * rows, rows), :] = left[0, a, window, :]
            flipped[:, :used] = out[a].T
            for level in range(depth):
                window = block_rows(me, core, 3, level, rows)
                picked[pl.ds(level * rows, rows), :used] = flipped[window, :used]
            last[a] = picked[:, :used].T
    for r in range(right.shape[1]):
        turned[r] = right[0, r].T


def early_kernel(sources, mine, other, *refs):
    lefts, sums, wave = refs[:len(GROUPS)], refs[len(GROUPS):2 * len(GROUPS)], refs[-1]
    half_sectors, rows = mine.shape[1], mine.shape[2]
    depth = mine.shape[0] // 3
    me, core = sources[0], sources[1]
    for j in range(wave.shape[0]):
        source = sources[2 + j]
        for level in range(depth):
            window = block_rows(me, core, 3, level, rows)
            wave[j, window, :] = jnp.zeros((rows, wave.shape[2]), wave.dtype)

        def unpack(blocks, from_core):
            for quarter in range(3):
                for level in range(depth):
                    block = blocks[quarter * depth + level, source % half_sectors]
                    wave[j, block_rows(me, from_core, quarter, level, rows), :] = block.astype(wave.dtype)

        @pl.when(source // half_sectors == core)
        def _():
            unpack(mine, core)

        @pl.when(source // half_sectors != core)
        def _():
            unpack(other, 1 - core)

    for left, out in zip(lefts, sums):
        for a in range(left.shape[0]):
            for j in range(wave.shape[0]):
                out[a * wave.shape[0] + j] = jnp.dot(
                    left[a].astype(BF16), wave[j].astype(BF16), preferred_element_type=F32
                )


def products(pairs, targets, live, early, left_last, wave_last, turned, outs, halves, total):
    ops_r, need = turned.shape[0], wave_last.shape[0]
    for a in range(left_last.shape[0]):
        for j in range(need):
            late = jnp.dot(left_last[a].astype(BF16), wave_last[j].astype(BF16), preferred_element_type=F32)
            halves[a * need + j] = (early[a * need + j] + late).astype(BF16)

    total[...] = jnp.zeros_like(total)
    for slot in range(pairs.shape[2]):
        code = pairs[0, 0, slot]
        target = jnp.where(slot < live[0, 0], targets[0, 0, slot], total.shape[0] - 1)
        total[target] += jnp.dot(halves[code // ops_r], turned[code % ops_r], preferred_element_type=F32)

    for i, out in enumerate(outs):
        depth, sec_dev, rows = out.shape[:3]
        for level in range(depth):
            for t in range(sec_dev):
                out[level, t] = total[t, pl.ds((i * depth + level) * rows, rows), :].astype(out.dtype)


def first_kernel(sources, pairs, targets, live, mine_last, other_last, early, left_last, turned,
                 wave_last, out, halves, total):
    depth, half_sectors, rows, size = mine_last.shape
    for j in range(wave_last.shape[0]):
        source = sources[2 + j]
        for owned, blocks in ((True, mine_last), (False, other_last)):
            @pl.when((source // half_sectors == sources[1]) == owned)
            def _(blocks=blocks):
                for level in range(depth):
                    block = blocks[level, source % half_sectors]
                    wave_last[j, pl.ds(level * rows, rows), :] = block.astype(wave_last.dtype)

    products(pairs, targets, live, early, left_last, wave_last, turned, [out], halves, total)


def next_kernel(pairs, targets, live, early, left_last, wave_last, turned, *refs):
    products(pairs, targets, live, early, left_last, wave_last, turned, refs[:-2], *refs[-2:])


def call(kernel, out_shapes, scratch_shapes, flops, *operands):
    def spec(array):
        return SMEM if jnp.issubdtype(array.dtype, jnp.integer) else VMEM

    return pl.pallas_call(
        kernel,
        out_shape=out_shapes,
        in_specs=[spec(operand) for operand in operands],
        out_specs=[spec(out) for out in out_shapes],
        scratch_shapes=scratch_shapes,
        compiler_params=pltpu.CompilerParams(vmem_limit_bytes=VMEM_BYTES),
        cost_estimate=pl.CostEstimate(flops=flops, bytes_accessed=2**20, transcendentals=0),
    )(*operands)


def on_device(terms, cores, wave_blocks, left_ops, right_ops, wanted, pairs, targets, live):
    sectors, rows, size = wave_blocks.shape
    me = lax.axis_index("term")
    core = lax.axis_index("sector") % 2
    depth = terms // 4
    sec_dev = sectors // cores
    ops_l, ops_r, need = left_ops.shape[1], right_ops.shape[1], wanted.shape[2]
    half = sectors // 2
    far_first = sorted(range(1, depth), key=lambda k: (k ^ (depth - 1)) & -2)
    quarter = depth * rows
    shape = jax.ShapeDtypeStruct

    def swap(array, near, level=0):
        def partner(t, c):
            return t ^ (near[c % 2] + 4 * level)
        pairs_of = [(t * cores + c, partner(t, c) * cores + c) for t in range(terms) for c in range(cores)]
        return lax.ppermute(array, AXES, pairs_of)

    none, first, second = (0, 0), (1, 2), (2, 1)
    across = [(t * cores + c, t * cores + (c ^ 1)) for t in range(terms) for c in range(cores)]

    work_type = BF16 if rows % 16 == 0 else F32
    used = [len(group) * quarter for group in GROUPS]
    place = jnp.stack([me, core]).astype(jnp.int32)
    *prepared, sources = call(
        functools.partial(prepare_kernel, rows),
        [shape((ops_l, u, size), work_type) for u in used]
        + [shape((ops_l, u, quarter), work_type) for u in used]
        + [shape((ops_r, size, size), BF16), shape((2 + need,), jnp.int32)],
        [pltpu.VMEM((size, max(used)), work_type), pltpu.VMEM((quarter, max(used)), work_type)],
        size**3, place, wanted, left_ops.astype(work_type), right_ops,
    )

    own = lax.dynamic_slice_in_dim(wave_blocks, core * half, half, 0)[None]
    by_level = {k: swap(own, none, k) for k in far_first}
    line = jnp.concatenate([own] + [by_level[k] for k in range(1, depth)], 0)
    line, prepared, sources = lax.optimization_barrier((line, prepared, sources))
    lefts, lasts, turned = prepared[:len(GROUPS)], prepared[len(GROUPS):-1], prepared[-1]
    from_first = swap(line, first)
    from_second = swap(line, second)
    mine_last = swap(from_first, second)
    mine = jnp.concatenate([line, from_first, from_second], 0)
    other = lax.ppermute(mine, AXES, across)
    early = call(
        early_kernel,
        [shape((ops_l * need, u, size), F32) for u in used],
        [pltpu.VMEM((need, size, size), work_type)],
        8 * size**3, sources, mine, other, *lefts,
    )
    mine_last, early = lax.optimization_barrier((mine_last, early))
    other_last = lax.ppermute(mine_last, AXES, across)

    def sums(kernel, group, extra, kinds, *operands):
        return call(
            kernel, extra + [shape((depth, sec_dev, rows, size), kind) for kind in kinds],
            [pltpu.VMEM((ops_l * need, used[group], size), BF16), pltpu.VMEM((sec_dev + 1, used[group], size), F32)],
            24 * used[group] * size**2, *operands,
        )

    wave_last, far = sums(
        first_kernel, 0, [shape((need, quarter, size), work_type)], (BF16,),
        sources, pairs, targets, live, mine_last, other_last, early[0], lasts[0], turned,
    )
    far = swap(far, first)
    near, = sums(next_kernel, 1, [], (BF16,), pairs, targets, live, early[1], lasts[1], wave_last, turned)
    near = swap(near, first)
    passing, keep = sums(next_kernel, 2, [], (F32, F32), pairs, targets, live, early[2], lasts[2], wave_last, turned)

    passing = (passing + far.astype(F32)).astype(BF16)
    pass_rest = swap(passing[1:], second)
    line_rest = (keep[1:] + near[1:].astype(F32) + pass_rest.astype(F32)).astype(BF16)
    line_rest, pass_own = lax.optimization_barrier((line_rest, passing[0]))
    arrived = [swap(line_rest[k - 1], none, k) for k in far_first]
    pass_own = swap(pass_own, second)
    sigma = keep[0] + near[0].astype(F32) + pass_own.astype(F32)
    for part in arrived:
        sigma = sigma + part.astype(F32)
    return sigma


def solution(mesh):
    return jax.shard_map(
        functools.partial(on_device, mesh.shape["term"], mesh.shape["sector"]),
        mesh=mesh,
        in_specs=(
            P(None, "term", None),
            P("sector", "term", None, None),
            P("sector", "term", None, None),
            P("sector", None, None),
            P("sector", "term", None),
            P("sector", "term", None),
            P("sector", "term"),
        ),
        out_specs=P("sector", "term", None),
        check_vma=False,
    )
```

```python
import functools
import math

import jax
import jax.numpy as jnp
from jax import lax
from jax.experimental import pallas as pl
from jax.experimental.pallas import tpu as pltpu
from jax.sharding import PartitionSpec as P

AXES = ("term", "sector")
BF16 = jnp.bfloat16
F32 = jnp.float32
VMEM = pl.BlockSpec(memory_space=pltpu.VMEM)
SMEM = pl.BlockSpec(memory_space=pltpu.SMEM)
SPARE_BYTES = 4 * 2**20
GROUPS = ((3,), (1,), (2, 0))


def block_rows(me, core, quarter, level, rows):
    near = jnp.where(core == 0, quarter, (0, 2, 1, 3)[quarter])
    owner = lax.bitwise_xor(me, near + 4 * level)
    return pl.ds(pl.multiple_of(owner * rows, rows), rows)


def prepare_kernel(rows, place, wanted, left, right, *refs):
    lefts, lasts = refs[:len(GROUPS)], refs[len(GROUPS):2 * len(GROUPS)]
    turned, sources, flipped, picked = refs[2 * len(GROUPS):]
    me, core = place[0], place[1]
    depth = left.shape[2] // (4 * rows)
    sources[0], sources[1] = me, core
    for j in range(wanted.shape[2]):
        sources[2 + j] = wanted[0, me, j]
    for a in range(left.shape[1]):
        for out, last, quarters in zip(lefts, lasts, GROUPS):
            used = out.shape[1]
            for i, quarter in enumerate(quarters):
                for level in range(depth):
                    window = block_rows(me, core, quarter, level, rows)
                    out[a, pl.ds((i * depth + level) * rows, rows), :] = left[0, a, window, :]
            flipped[:, :used] = out[a].T
            for level in range(depth):
                window = block_rows(me, core, 3, level, rows)
                picked[pl.ds(level * rows, rows), :used] = flipped[window, :used]
            last[a] = picked[:, :used].T
    for r in range(right.shape[1]):
        turned[r] = right[0, r].T


def early_kernel(sources, mine, other, *refs):
    lefts, sums, wave = refs[:len(GROUPS)], refs[len(GROUPS):2 * len(GROUPS)], refs[-1]
    half_sectors, rows = mine.shape[1], mine.shape[2]
    depth = mine.shape[0] // 3
    me, core = sources[0], sources[1]
    for j in range(wave.shape[0]):
        source = sources[2 + j]
        for level in range(depth):
            window = block_rows(me, core, 3, level, rows)
            wave[j, window, :] = jnp.zeros((rows, wave.shape[2]), wave.dtype)

        def unpack(blocks, from_core):
            for quarter in range(3):
                for level in range(depth):
                    block = blocks[quarter * depth + level, source % half_sectors]
                    wave[j, block_rows(me, from_core, quarter, level, rows), :] = block.astype(wave.dtype)

        @pl.when(source // half_sectors == core)
        def _():
            unpack(mine, core)

        @pl.when(source // half_sectors != core)
        def _():
            unpack(other, 1 - core)

    for left, out in zip(lefts, sums):
        for a in range(left.shape[0]):
            for j in range(wave.shape[0]):
                out[a * wave.shape[0] + j] = jnp.dot(
                    left[a].astype(BF16), wave[j].astype(BF16), preferred_element_type=F32
                )


def products(pairs, targets, live, early, left_last, wave_last, turned, outs, halves, total):
    ops_r, need = turned.shape[0], wave_last.shape[0]
    for a in range(left_last.shape[0]):
        for j in range(need):
            late = jnp.dot(left_last[a].astype(BF16), wave_last[j].astype(BF16), preferred_element_type=F32)
            halves[a * need + j] = (early[a * need + j] + late).astype(BF16)

    total[...] = jnp.zeros_like(total)
    for slot in range(pairs.shape[2]):
        code = pairs[0, 0, slot]
        target = jnp.where(slot < live[0, 0], targets[0, 0, slot], total.shape[0] - 1)
        total[target] += jnp.dot(halves[code // ops_r], turned[code % ops_r], preferred_element_type=F32)

    for i, out in enumerate(outs):
        depth, sec_dev, rows = out.shape[:3]
        for level in range(depth):
            for t in range(sec_dev):
                out[level, t] = total[t, pl.ds((i * depth + level) * rows, rows), :].astype(out.dtype)


def first_kernel(sources, pairs, targets, live, mine_last, other_last, early, left_last, turned,
                 wave_last, out, halves, total):
    depth, half_sectors, rows, size = mine_last.shape
    for j in range(wave_last.shape[0]):
        source = sources[2 + j]
        for owned, blocks in ((True, mine_last), (False, other_last)):
            @pl.when((source // half_sectors == sources[1]) == owned)
            def _(blocks=blocks):
                for level in range(depth):
                    block = blocks[level, source % half_sectors]
                    wave_last[j, pl.ds(level * rows, rows), :] = block.astype(wave_last.dtype)

    products(pairs, targets, live, early, left_last, wave_last, turned, [out], halves, total)


def next_kernel(pairs, targets, live, early, left_last, wave_last, turned, *refs):
    products(pairs, targets, live, early, left_last, wave_last, turned, refs[:-2], *refs[-2:])


def call(kernel, out_shapes, scratch_shapes, flops, *operands):
    def spec(array):
        return SMEM if jnp.issubdtype(array.dtype, jnp.integer) else VMEM

    held = [*operands, *out_shapes, *scratch_shapes]
    need_bytes = sum(math.prod(array.shape) * jnp.dtype(array.dtype).itemsize for array in held)
    return pl.pallas_call(
        kernel,
        out_shape=out_shapes,
        in_specs=[spec(operand) for operand in operands],
        out_specs=[spec(out) for out in out_shapes],
        scratch_shapes=scratch_shapes,
        compiler_params=pltpu.CompilerParams(vmem_limit_bytes=need_bytes + SPARE_BYTES),
        cost_estimate=pl.CostEstimate(flops=flops, bytes_accessed=2**20, transcendentals=0),
    )(*operands)


def on_device(terms, cores, wave_blocks, left_ops, right_ops, wanted, pairs, targets, live):
    sectors, rows, size = wave_blocks.shape
    me = lax.axis_index("term")
    core = lax.axis_index("sector") % 2
    depth = terms // 4
    sec_dev = sectors // cores
    ops_l, ops_r, need = left_ops.shape[1], right_ops.shape[1], wanted.shape[2]
    half = sectors // 2
    far_first = sorted(range(1, depth), key=lambda k: (k ^ (depth - 1)) & -2)
    quarter = depth * rows
    shape = jax.ShapeDtypeStruct

    def swap(array, near, level=0):
        def partner(t, c):
            return t ^ (near[c % 2] + 4 * level)
        pairs_of = [(t * cores + c, partner(t, c) * cores + c) for t in range(terms) for c in range(cores)]
        return lax.ppermute(array, AXES, pairs_of)

    none, first, second = (0, 0), (1, 2), (2, 1)
    across = [(t * cores + c, t * cores + (c ^ 1)) for t in range(terms) for c in range(cores)]

    work_type = BF16 if rows % 16 == 0 else F32
    used = [len(group) * quarter for group in GROUPS]
    own = lax.dynamic_slice_in_dim(wave_blocks, core * half, half, 0)[None]
    by_level = {k: swap(own, none, k) for k in far_first}
    line = jnp.concatenate([own] + [by_level[k] for k in range(1, depth)], 0)
    place = jnp.stack([me, core]).astype(jnp.int32)
    place, line = lax.optimization_barrier((place, line))
    *prepared, sources = call(
        functools.partial(prepare_kernel, rows),
        [shape((ops_l, u, size), work_type) for u in used]
        + [shape((ops_l, u, quarter), work_type) for u in used]
        + [shape((ops_r, size, size), BF16), shape((2 + need,), jnp.int32)],
        [pltpu.VMEM((size, max(used)), work_type), pltpu.VMEM((quarter, max(used)), work_type)],
        size**3, place, wanted, left_ops.astype(work_type), right_ops,
    )
    from_first = swap(line, first)
    from_second = swap(line, second)
    from_first, from_second, prepared, sources = lax.optimization_barrier((from_first, from_second, prepared, sources))
    lefts, lasts, turned = prepared[:len(GROUPS)], prepared[len(GROUPS):-1], prepared[-1]
    mine_last = swap(from_first, second)
    mine = jnp.concatenate([line, from_first, from_second], 0)
    other = lax.ppermute(mine, AXES, across)
    early = call(
        early_kernel,
        [shape((ops_l * need, u, size), F32) for u in used],
        [pltpu.VMEM((need, size, size), work_type)],
        8 * size**3, sources, mine, other, *lefts,
    )
    mine_last, early = lax.optimization_barrier((mine_last, early))
    other_last = lax.ppermute(mine_last, AXES, across)

    def sums(kernel, group, extra, kinds, *operands):
        return call(
            kernel, extra + [shape((depth, sec_dev, rows, size), kind) for kind in kinds],
            [pltpu.VMEM((ops_l * need, used[group], size), BF16), pltpu.VMEM((sec_dev + 1, used[group], size), F32)],
            24 * used[group] * size**2, *operands,
        )

    wave_last, far = sums(
        first_kernel, 0, [shape((need, quarter, size), work_type)], (BF16,),
        sources, pairs, targets, live, mine_last, other_last, early[0], lasts[0], turned,
    )
    far = swap(far, first)
    near, = sums(next_kernel, 1, [], (BF16,), pairs, targets, live, early[1], lasts[1], wave_last, turned)
    near = swap(near, first)
    passing, keep = sums(next_kernel, 2, [], (F32, F32), pairs, targets, live, early[2], lasts[2], wave_last, turned)

    passing = (passing + far.astype(F32)).astype(BF16)
    pass_rest = swap(passing[1:], second)
    line_rest = (keep[1:] + near[1:].astype(F32) + pass_rest.astype(F32)).astype(BF16)
    line_rest, pass_own = lax.optimization_barrier((line_rest, passing[0]))
    arrived = [swap(line_rest[k - 1], none, k) for k in far_first]
    pass_own = swap(pass_own, second)
    sigma = keep[0] + near[0].astype(F32) + pass_own.astype(F32)
    for part in arrived:
        sigma = sigma + part.astype(F32)
    return sigma


def solution(mesh):
    return jax.shard_map(
        functools.partial(on_device, mesh.shape["term"], mesh.shape["sector"]),
        mesh=mesh,
        in_specs=(
            P(None, "term", None),
            P("sector", "term", None, None),
            P("sector", "term", None, None),
            P("sector", None, None),
            P("sector", "term", None),
            P("sector", "term", None),
            P("sector", "term"),
        ),
        out_specs=P("sector", "term", None),
        check_vma=False,
    )
```

```python
import functools
import math

import jax
import jax.numpy as jnp
from jax import lax
from jax.experimental import pallas as pl
from jax.experimental.pallas import tpu as pltpu
from jax.sharding import PartitionSpec as P

AXES = ("term", "sector")
BF16 = jnp.bfloat16
F32 = jnp.float32
VMEM = pl.BlockSpec(memory_space=pltpu.VMEM)
SMEM = pl.BlockSpec(memory_space=pltpu.SMEM)
SPARE_BYTES = 4 * 2**20
GROUPS = ((3,), (1,), (2,), (0,))


def block_rows(me, core, quarter, level, rows):
    near = jnp.where(core == 0, quarter, (0, 2, 1, 3)[quarter])
    owner = lax.bitwise_xor(me, near + 4 * level)
    return pl.ds(pl.multiple_of(owner * rows, rows), rows)


def prepare_kernel(rows, place, wanted, left, right, *refs):
    lefts, lasts = refs[:len(GROUPS)], refs[len(GROUPS):2 * len(GROUPS)]
    turned, sources, flipped, picked = refs[2 * len(GROUPS):]
    me, core = place[0], place[1]
    depth = left.shape[2] // (4 * rows)
    sources[0], sources[1] = me, core
    for j in range(wanted.shape[2]):
        sources[2 + j] = wanted[0, me, j]
    for a in range(left.shape[1]):
        for out, last, quarters in zip(lefts, lasts, GROUPS):
            used = out.shape[1]
            for i, quarter in enumerate(quarters):
                for level in range(depth):
                    window = block_rows(me, core, quarter, level, rows)
                    out[a, pl.ds((i * depth + level) * rows, rows), :] = left[0, a, window, :]
            flipped[:, :used] = out[a].T
            for level in range(depth):
                window = block_rows(me, core, 3, level, rows)
                picked[pl.ds(level * rows, rows), :used] = flipped[window, :used]
            last[a] = picked[:, :used].T
    for r in range(right.shape[1]):
        turned[r] = right[0, r].T


def early_kernel(sources, mine, other, *refs):
    lefts, sums, wave = refs[:len(GROUPS)], refs[len(GROUPS):2 * len(GROUPS)], refs[-1]
    half_sectors, rows = mine.shape[1], mine.shape[2]
    depth = mine.shape[0] // 3
    me, core = sources[0], sources[1]
    for j in range(wave.shape[0]):
        source = sources[2 + j]
        for level in range(depth):
            window = block_rows(me, core, 3, level, rows)
            wave[j, window, :] = jnp.zeros((rows, wave.shape[2]), wave.dtype)

        def unpack(blocks, from_core):
            for quarter in range(3):
                for level in range(depth):
                    block = blocks[quarter * depth + level, source % half_sectors]
                    wave[j, block_rows(me, from_core, quarter, level, rows), :] = block.astype(wave.dtype)

        @pl.when(source // half_sectors == core)
        def _():
            unpack(mine, core)

        @pl.when(source // half_sectors != core)
        def _():
            unpack(other, 1 - core)

    for left, out in zip(lefts, sums):
        for a in range(left.shape[0]):
            for j in range(wave.shape[0]):
                out[a * wave.shape[0] + j] = jnp.dot(
                    left[a].astype(BF16), wave[j].astype(BF16), preferred_element_type=F32
                )


def products(pairs, targets, live, early, left_last, wave_last, turned, outs, halves, total):
    ops_r, need = turned.shape[0], wave_last.shape[0]
    for a in range(left_last.shape[0]):
        for j in range(need):
            late = jnp.dot(left_last[a].astype(BF16), wave_last[j].astype(BF16), preferred_element_type=F32)
            halves[a * need + j] = (early[a * need + j] + late).astype(BF16)

    total[...] = jnp.zeros_like(total)
    for slot in range(pairs.shape[2]):
        code = pairs[0, 0, slot]
        target = jnp.where(slot < live[0, 0], targets[0, 0, slot], total.shape[0] - 1)
        total[target] += jnp.dot(halves[code // ops_r], turned[code % ops_r], preferred_element_type=F32)

    for i, out in enumerate(outs):
        depth, sec_dev, rows = out.shape[:3]
        for level in range(depth):
            for t in range(sec_dev):
                out[level, t] = total[t, pl.ds((i * depth + level) * rows, rows), :].astype(out.dtype)


def first_kernel(sources, pairs, targets, live, mine_last, other_last, early, left_last, turned,
                 wave_last, out, halves, total):
    depth, half_sectors, rows, size = mine_last.shape
    for j in range(wave_last.shape[0]):
        source = sources[2 + j]
        for owned, blocks in ((True, mine_last), (False, other_last)):
            @pl.when((source // half_sectors == sources[1]) == owned)
            def _(blocks=blocks):
                for level in range(depth):
                    block = blocks[level, source % half_sectors]
                    wave_last[j, pl.ds(level * rows, rows), :] = block.astype(wave_last.dtype)

    products(pairs, targets, live, early, left_last, wave_last, turned, [out], halves, total)


def next_kernel(pairs, targets, live, early, left_last, wave_last, turned, *refs):
    products(pairs, targets, live, early, left_last, wave_last, turned, refs[:-2], *refs[-2:])


def call(kernel, out_shapes, scratch_shapes, flops, *operands):
    def spec(array):
        return SMEM if jnp.issubdtype(array.dtype, jnp.integer) else VMEM

    held = [*operands, *out_shapes, *scratch_shapes]
    need_bytes = sum(math.prod(array.shape) * jnp.dtype(array.dtype).itemsize for array in held)
    return pl.pallas_call(
        kernel,
        out_shape=out_shapes,
        in_specs=[spec(operand) for operand in operands],
        out_specs=[spec(out) for out in out_shapes],
        scratch_shapes=scratch_shapes,
        compiler_params=pltpu.CompilerParams(vmem_limit_bytes=need_bytes + SPARE_BYTES),
        cost_estimate=pl.CostEstimate(flops=flops, bytes_accessed=2**20, transcendentals=0),
    )(*operands)


def on_device(terms, cores, wave_blocks, left_ops, right_ops, wanted, pairs, targets, live):
    sectors, rows, size = wave_blocks.shape
    me = lax.axis_index("term")
    core = lax.axis_index("sector") % 2
    depth = terms // 4
    sec_dev = sectors // cores
    ops_l, ops_r, need = left_ops.shape[1], right_ops.shape[1], wanted.shape[2]
    half = sectors // 2
    far_first = sorted(range(1, depth), key=lambda k: (k ^ (depth - 1)) & -2)
    quarter = depth * rows
    shape = jax.ShapeDtypeStruct

    def swap(array, near, level=0):
        def partner(t, c):
            return t ^ (near[c % 2] + 4 * level)
        pairs_of = [(t * cores + c, partner(t, c) * cores + c) for t in range(terms) for c in range(cores)]
        return lax.ppermute(array, AXES, pairs_of)

    none, first, second = (0, 0), (1, 2), (2, 1)
    across = [(t * cores + c, t * cores + (c ^ 1)) for t in range(terms) for c in range(cores)]

    work_type = BF16 if rows % 16 == 0 else F32
    used = [len(group) * quarter for group in GROUPS]
    own = lax.dynamic_slice_in_dim(wave_blocks, core * half, half, 0)[None]
    by_level = {k: swap(own, none, k) for k in far_first}
    line = jnp.concatenate([own] + [by_level[k] for k in range(1, depth)], 0)
    place = jnp.stack([me, core]).astype(jnp.int32)
    place, line = lax.optimization_barrier((place, line))
    *prepared, sources = call(
        functools.partial(prepare_kernel, rows),
        [shape((ops_l, u, size), work_type) for u in used]
        + [shape((ops_l, u, quarter), work_type) for u in used]
        + [shape((ops_r, size, size), BF16), shape((2 + need,), jnp.int32)],
        [pltpu.VMEM((size, max(used)), work_type), pltpu.VMEM((quarter, max(used)), work_type)],
        size**3, place, wanted, left_ops.astype(work_type), right_ops,
    )
    from_first = swap(line, first)
    from_second = swap(line, second)
    from_first, from_second, prepared, sources = lax.optimization_barrier((from_first, from_second, prepared, sources))
    lefts, lasts, turned = prepared[:len(GROUPS)], prepared[len(GROUPS):-1], prepared[-1]
    mine_last = swap(from_first, second)
    mine = jnp.concatenate([line, from_first, from_second], 0)
    other = lax.ppermute(mine, AXES, across)
    early = call(
        early_kernel,
        [shape((ops_l * need, u, size), F32) for u in used],
        [pltpu.VMEM((need, size, size), work_type)],
        8 * size**3, sources, mine, other, *lefts,
    )
    mine_last, early = lax.optimization_barrier((mine_last, early))
    other_last = lax.ppermute(mine_last, AXES, across)

    def sums(kernel, group, extra, kinds, *operands):
        return call(
            kernel, extra + [shape((depth, sec_dev, rows, size), kind) for kind in kinds],
            [pltpu.VMEM((ops_l * need, used[group], size), BF16), pltpu.VMEM((sec_dev + 1, used[group], size), F32)],
            24 * used[group] * size**2, *operands,
        )

    wave_last, far = sums(
        first_kernel, 0, [shape((need, quarter, size), work_type)], (BF16,),
        sources, pairs, targets, live, mine_last, other_last, early[0], lasts[0], turned,
    )
    far = swap(far, first)
    near, = sums(next_kernel, 1, [], (BF16,), pairs, targets, live, early[1], lasts[1], wave_last, turned)
    near = swap(near, first)
    passing, = sums(next_kernel, 2, [], (F32,), pairs, targets, live, early[2], lasts[2], wave_last, turned)

    passing = (passing + far.astype(F32)).astype(BF16)
    pass_rest, wave_last = lax.optimization_barrier((passing[1:], wave_last))
    pass_rest = swap(pass_rest, second)
    keep, = sums(next_kernel, 3, [], (F32,), pairs, targets, live, early[3], lasts[3], wave_last, turned)
    line_rest = (keep[1:] + near[1:].astype(F32) + pass_rest.astype(F32)).astype(BF16)
    line_rest, pass_own = lax.optimization_barrier((line_rest, passing[0]))
    arrived = [swap(line_rest[k - 1], none, k) for k in far_first]
    pass_own = swap(pass_own, second)
    sigma = keep[0] + near[0].astype(F32) + pass_own.astype(F32)
    for part in arrived:
        sigma = sigma + part.astype(F32)
    return sigma


def solution(mesh):
    return jax.shard_map(
        functools.partial(on_device, mesh.shape["term"], mesh.shape["sector"]),
        mesh=mesh,
        in_specs=(
            P(None, "term", None),
            P("sector", "term", None, None),
            P("sector", "term", None, None),
            P("sector", None, None),
            P("sector", "term", None),
            P("sector", "term", None),
            P("sector", "term"),
        ),
        out_specs=P("sector", "term", None),
        check_vma=False,
    )
```
